256 devices in a mesh: row: 8 (over y_hi, x), col: 32 (over y_lo, z, core).
Axes of the slice: x: 4, y: 4 (y_hi: 2, y_lo: 2; y = y_hi * 2 + y_lo), z: 8, core: 2. Of those that a mesh axis runs over, the one named last changes fastest.
Arguments:
- messages: bfloat16 [8, 32, 1024, 512], P('row', 'col'), may hold values from -6 to 6
- targets: int32 [8, 32, 1024], P('row', 'col'), may hold values from 0 to 511
- reverse_rows: int32 [8, 32, 8, 128], P('row', 'col'), may hold values from 0 to 127, as said below
- nodes: bfloat16 [32, 512, 512], P('col', 'row'), may hold values from -6 to 6
- w_in: bfloat16 [2, 1536, 512], replicated, may hold values from -0.15625 to 0.15625
- w_res: bfloat16 [2, 2, 2, 512, 512], replicated, may hold values from -0.25 to 0.25
- w_node: bfloat16 [2, 512, 512], replicated, may hold values from -0.25 to 0.25
Outputs:
- edge_out: bfloat16 [8, 32, 1024, 512], P('row', 'col')
- node_out: bfloat16 [32, 512, 512], P('col', 'row')
The draws below stay inside these ranges and needn't reach their ends.
Inputs may be any that keep to these rules, and one draw needn't show every extreme that they name: reverse_rows[s, c, k] is a permutation of the block's rows, and the reversal is an involution: the reversed edge of the reversed edge is the edge itself.
All inputs are finite; a program needn't handle non-finite values.
Results may differ from the reference program's by a relative error of at most 0.0065.
Values may be sent and summed in bfloat16 or wider, within the bound.
A program may use at most 64 MiB of HBM per device.

```python
import math
import jax
import jax.numpy as jnp
from jax import lax

D = 512
BLOCK = 128
NBLK = 8
ITERS = 2
NODES_DEV = 64
EDGES_DEV = 1024
SLABS = 8
GROUPS = 32
NODES = 512


def draw_reverse_rows(key, part):
    key_list = jax.random.split(jax.random.fold_in(key, 4711), SLABS * GROUPS * 4)
    perms = jax.vmap(lambda one_key: jax.random.permutation(one_key, BLOCK))(key_list)
    perms = perms.reshape(SLABS, GROUPS, 4, BLOCK).astype(jnp.int32)
    inverse = jnp.argsort(perms, axis=-1, stable=True).astype(jnp.int32)
    result = [perms[:, :, 0], inverse[:, :, 0]]
    for offset in range(1, 4):
        result.append(perms[:, :, offset])
        result.append(jnp.roll(inverse[:, :, offset], offset, axis=1))
    return jnp.stack(result, axis=2).astype(jnp.int32)


def plant(entries, own_key, least, high):
    longest = entries.shape.index(max(entries.shape))
    spots = []
    for shift in (0, 1):
        where = [jax.random.randint(jax.random.fold_in(own_key, axis), (), 0, length) for axis, length in enumerate(entries.shape)]
        where[longest] = (where[longest] + shift) % entries.shape[longest]
        spots.append(tuple(where))
    return entries.at[spots[0]].set(least).at[spots[1]].set(high)


def block_levels(key, shape, pieces, low, largest):
    factor_of = 1.0
    for dim, blocks in pieces:
        draws = jax.random.uniform(jax.random.fold_in(jax.random.fold_in(key, 6), dim), (blocks,), jnp.float32, low / len(pieces), largest / len(pieces))
        factor_of = factor_of * jnp.repeat(jnp.exp(draws), shape[dim] // blocks).reshape((-1,) + (1,) * (len(shape) - 1 - dim))
    return factor_of


def bell_draw(rng, extent, scale, most, shards=(), held_as=jnp.bfloat16):
    level = block_levels(rng, extent, shards, -0.22, 0.18) if shards else 1.0
    entries = jax.random.normal(rng, extent, jnp.float32) * scale * level
    return jnp.minimum(jnp.maximum(entries, -most), most).astype(held_as)


def setup_inputs(seed: int = 0) -> dict:
    seeds = jax.random.split(jax.random.key(seed), 8)
    messages = bell_draw(seeds[0], (SLABS, GROUPS, EDGES_DEV, D), 1.0, 6.0, ((0, 8), (1, 32)))
    targets = plant(jax.random.randint(seeds[1], (SLABS, GROUPS, EDGES_DEV), 0, NODES), jax.random.fold_in(seeds[1], 1), 0, NODES - 1).astype(jnp.int32)
    reverse_rows = draw_reverse_rows(jax.random.fold_in(seeds[7], 71), 0)
    nodes = bell_draw(seeds[3], (GROUPS, NODES, D), 1.0, 6.0, ((0, 32), (1, 8)))
    w_in = bell_draw(seeds[4], (ITERS, 3 * D, D), (3 * D) ** -0.5, 0.15625)
    w_res = bell_draw(seeds[5], (ITERS, 2, 2, D, D), D ** -0.5, 0.25)
    w_node = bell_draw(seeds[6], (ITERS, D, D), D ** -0.5, 0.25)
    return {"messages": messages, "targets": targets, "reverse_rows": reverse_rows, "nodes": nodes, "w_in": w_in, "w_res": w_res, "w_node": w_node}


OFFSETS = (0, 0, 1, -1, 2, -2, 3, -3)
ROOT_HALF = 0.7071067811865476

def reverse_all(stack, reverse_rows):
    blocks = stack.reshape(SLABS, GROUPS, NBLK, BLOCK, stack.shape[-1])
    result = []
    for index in range(NBLK):
        source = jnp.roll(blocks[:, :, index ^ 1], -OFFSETS[index], axis=1)
        row_order = reverse_rows[:, :, index, :].astype(jnp.int32)
        result.append(jnp.take_along_axis(source, row_order[:, :, :, None], axis=2))
    return jnp.stack(result, axis=2).reshape(stack.shape)

def edge_layer(m_rev, h_src, h_tgt, current, w_first, w_blocks):
    joined = jnp.concatenate([m_rev, h_src, h_tgt], axis=-1)
    hidden = jax.nn.silu(jnp.dot(joined, w_first, preferred_element_type=jnp.float32)).astype(jnp.bfloat16)
    summed = hidden.astype(jnp.float32)
    for index in range(2):
        inner_act = jax.nn.silu(jnp.dot(hidden, w_blocks[index, 0], preferred_element_type=jnp.float32)).astype(jnp.bfloat16)
        summed = (hidden.astype(jnp.float32) + jax.nn.silu(jnp.dot(inner_act, w_blocks[index, 1], preferred_element_type=jnp.float32))) * ROOT_HALF
        if index == 0:
            hidden = summed.astype(jnp.bfloat16)
    return ((current.astype(jnp.float32) + summed) * ROOT_HALF).astype(jnp.bfloat16)

def reference(messages, targets, reverse_rows, nodes, w_in, w_res, w_node):
    agg_scale = 1.0 / math.sqrt(EDGES_DEV // NODES_DEV)
    current = messages
    node_flat = nodes.reshape(GROUPS * NODES, D)
    group_ids = (targets + (jnp.arange(GROUPS, dtype=jnp.int32) * NODES)[None, :, None]).astype(jnp.int32)

    def add_slab(running, pair):
        slab_rows, slab_ids = pair
        return (running + jax.ops.segment_sum(slab_rows.reshape(-1, D).astype(jnp.float32), slab_ids.reshape(-1), num_segments=GROUPS * NODES), None)
    for layer in range(ITERS):
        gathered_sum, _ = lax.scan(add_slab, jnp.zeros((GROUPS * NODES, D), jnp.float32), (current, group_ids))
        scaled = (gathered_sum * agg_scale).astype(jnp.bfloat16)
        update = jax.nn.silu(jnp.dot(scaled, w_node[layer], preferred_element_type=jnp.float32))
        node_flat = (node_flat.astype(jnp.float32) + update).astype(jnp.bfloat16)
        h_tgt = jnp.take(node_flat, group_ids, axis=0)
        m_rev = reverse_all(current, reverse_rows)
        h_src = reverse_all(h_tgt, reverse_rows)
        w_first = w_in[layer]
        w_blocks = w_res[layer]

        def slab_layer(items):
            return edge_layer(items[0], items[1], items[2], items[3], w_first, w_blocks)
        current = lax.map(slab_layer, (m_rev, h_src, h_tgt, current))
    return (current, node_flat.reshape(GROUPS, NODES, D))
```

```python
import functools
import math

import jax
import jax.numpy as jnp
from jax import lax
from jax.experimental import pallas as pl
from jax.experimental.pallas import tpu as pltpu
from jax.sharding import PartitionSpec as P

OFFSETS = (0, 0, 1, -1, 2, -2, 3, -3)
ROOT_HALF = 0.7071067811865476
MESH = pl.DeviceIdType.MESH
F32 = jnp.float32
BF16 = jnp.bfloat16


def silu(v):
    half = 0.5 * v
    return half + half * jnp.tanh(half)


def mm(a, b):
    return jnp.dot(a, b, preferred_element_type=F32)


def kernel(
    rows_n,
    cols_n,
    msg,
    tgt,
    rev,
    node,
    w_in_hbm,
    w_res_hbm,
    w_node_hbm,
    edge_out,
    node_out,
    w_in,
    w_res,
    w_node,
    cur,
    onehot,
    perm,
    base,
    own_part,
    h_tgt,
    pre,
    h_own,
    h_all,
    part_out,
    part_in,
    u_out,
    u_in,
    w_sem,
    rs_send,
    rs_recv,
    ag_send,
    ag_recv,
    col_send,
    col_recv,
    out_sem,
):
    r, c = lax.axis_index("row"), lax.axis_index("col")
    edges, feat = msg.shape
    share = node.shape[0]
    points = share * rows_n
    block = edges // len(OFFSETS)
    pair = 2 * block
    agg_scale = 1.0 / math.sqrt(edges // share)
    layers = w_in_hbm.shape[0]

    def row_peer(j):
        return lax.rem(r + j, rows_n)

    def col_peer(offset):
        return lax.rem(c + offset + cols_n, cols_n)

    barrier = pltpu.get_barrier_semaphore()
    for j in range(1, rows_n):
        pl.semaphore_signal(barrier, inc=1, device_id=(row_peer(j), c), device_id_type=MESH)
    for off in OFFSETS[2:]:
        pl.semaphore_signal(barrier, inc=1, device_id=(r, col_peer(off)), device_id_type=MESH)

    loads = []
    for t in range(layers):
        for i, (src, dst) in enumerate(
            ((w_in_hbm, w_in), (w_node_hbm, w_node), (w_res_hbm, w_res))
        ):
            loads.append(pltpu.make_async_copy(src.at[t], dst.at[t], w_sem.at[t, i]))
            loads[-1].start()

    def rs_copy(t, j):
        return pltpu.make_async_remote_copy(
            src_ref=part_out.at[t, j - 1],
            dst_ref=part_in.at[t, j - 1],
            send_sem=rs_send.at[t, j - 1],
            recv_sem=rs_recv.at[t, j - 1],
            device_id=(row_peer(j), c),
            device_id_type=MESH,
        )

    def ag_copy(t, j):
        mine = pl.ds(pl.multiple_of(r * share, share), share)
        return pltpu.make_async_remote_copy(
            src_ref=h_all.at[t, mine],
            dst_ref=h_all.at[t, mine],
            send_sem=ag_send.at[t, j - 1],
            recv_sem=ag_recv.at[t, j - 1],
            device_id=(row_peer(j), c),
            device_id_type=MESH,
        )

    def ag_arrival(t, j):
        theirs = pl.ds(pl.multiple_of(row_peer(rows_n - j) * share, share), share)
        return pltpu.make_async_remote_copy(
            src_ref=h_all.at[t, theirs],
            dst_ref=h_all.at[t, theirs],
            send_sem=ag_send.at[t, j - 1],
            recv_sem=ag_recv.at[t, j - 1],
            device_id=(row_peer(j), c),
            device_id_type=MESH,
        )

    def col_copy(t, b):
        return pltpu.make_async_remote_copy(
            src_ref=u_out.at[t, b],
            dst_ref=u_in.at[t, (b ^ 1) - 2],
            send_sem=col_send.at[t, b - 2],
            recv_sem=col_recv.at[t, (b ^ 1) - 2],
            device_id=(r, col_peer(OFFSETS[b])),
            device_id_type=MESH,
        )

    def col_arrival(t, k):
        return pltpu.make_async_remote_copy(
            src_ref=u_out.at[t, k],
            dst_ref=u_in.at[t, k - 2],
            send_sem=col_send.at[t, k - 2],
            recv_sem=col_recv.at[t, k - 2],
            device_id=(r, col_peer(OFFSETS[k])),
            device_id_type=MESH,
        )

    def send_parts(t, messages):
        half = points // 2
        per = rows_n // 2
        for part in range(2):
            first = lax.rem(r + 1 + part * per, rows_n) * share
            ids = lax.rem(lax.broadcasted_iota(jnp.int32, (half, edges), 0) + first, points)
            hot = jnp.where(tgt[...] == ids, 1.0, 0.0).astype(BF16)
            sums = mm(hot, messages[...])
            for i in range(per):
                j = part * per + i + 1
                rows = sums[i * share : (i + 1) * share]
                if j == rows_n:
                    own_part[...] = rows
                    continue
                part_out[t, j - 1] = rows.astype(BF16)
                if t == 0 and j == 1:
                    pl.semaphore_wait(barrier, rows_n - 1 + len(OFFSETS) - 2)
                rs_copy(t, j).start()

    send_parts(0, msg)

    lane = lax.broadcasted_iota(jnp.int32, (block, block), 1)
    for k in range(len(OFFSETS)):
        rows = pl.ds(k * block, block)
        ids = jnp.broadcast_to(tgt[0:1, k * block : (k + 1) * block], (block, block)).T
        for i in range(points // block):
            onehot[rows, i * block : (i + 1) * block] = jnp.where(
                ids == lane + i * block, 1.0, 0.0
            ).astype(BF16)
        ids = jnp.broadcast_to(rev[k : k + 1, :], (block, block)).T
        perm[k] = jnp.where(ids == lane, 1.0, 0.0).astype(BF16)

    h_own[...] = node[...]
    for t in range(layers):
        last = t == layers - 1
        held = msg if t == 0 else cur
        loads[3 * t].wait()
        for q in range(edges // pair):
            rows = pl.ds(q * pair, pair)
            base[rows] = mm(held[rows], w_in[t, :feat])

        loads[3 * t + 1].wait()
        total = own_part[...]
        for j in range(1, rows_n):
            rs_copy(t, j).wait_recv()
            total = total + part_in[t, j - 1].astype(F32)
        scaled = (total * agg_scale).astype(BF16)
        h_new = (h_own[...].astype(F32) + silu(mm(scaled, w_node[t]))).astype(BF16)
        h_own[...] = h_new
        h_all[t, pl.ds(pl.multiple_of(r * share, share), share)] = h_new
        for j in range(1, rows_n):
            ag_copy(t, j).start()
        if last:
            node_copy = pltpu.make_async_copy(h_own, node_out, out_sem.at[edges // pair])
            node_copy.start()
        for j in range(1, rows_n):
            ag_arrival(t, j).wait_recv()

        for q in (3, 2, 1, 0):
            rows = pl.ds(q * pair, pair)
            picked = mm(onehot[rows], h_all[t]).astype(BF16)
            h_tgt[rows] = picked
            u = (base[rows] + mm(picked, w_in[t, feat : 2 * feat])).astype(BF16)
            for i in range(2):
                b = 2 * q + i
                u_out[t, b] = u[i * block : (i + 1) * block]
                if q:
                    col_copy(t, b).start()
        for q in (0, 1, 2, 3):
            rows = pl.ds(q * pair, pair)
            pre[rows] = mm(h_tgt[rows], w_in[t, 2 * feat :])

        loads[3 * t + 2].wait()
        for q in (0, 1, 2, 3):
            rows = pl.ds(q * pair, pair)
            moved = []
            for k in (2 * q, 2 * q + 1):
                if q:
                    col_arrival(t, k).wait_recv()
                    moved.append(mm(perm[k], u_in[t, k - 2]))
                else:
                    moved.append(mm(perm[k], u_out[t, k ^ 1]))
            hidden = silu(pre[rows] + jnp.concatenate(moved, axis=0)).astype(BF16)
            inner = silu(mm(hidden, w_res[t, 0, 0])).astype(BF16)
            hidden = (
                (hidden.astype(F32) + silu(mm(inner, w_res[t, 0, 1]))) * ROOT_HALF
            ).astype(BF16)
            inner = silu(mm(hidden, w_res[t, 1, 0])).astype(BF16)
            summed = (hidden.astype(F32) + silu(mm(inner, w_res[t, 1, 1]))) * ROOT_HALF
            cur[rows] = ((held[rows].astype(F32) + summed) * ROOT_HALF).astype(BF16)
            if last:
                pltpu.make_async_copy(cur.at[rows], edge_out.at[rows], out_sem.at[q]).start()
        if not last:
            send_parts(t + 1, cur)

    for t in range(layers):
        for j in range(1, rows_n):
            rs_copy(t, j).wait_send()
            ag_copy(t, j).wait_send()
        for b in range(2, len(OFFSETS)):
            col_copy(t, b).wait_send()
    for q in range(edges // pair):
        rows = pl.ds(q * pair, pair)
        pltpu.make_async_copy(cur.at[rows], edge_out.at[rows], out_sem.at[q]).wait()
    node_copy.wait()


def shards(rows_n, cols_n, messages, targets, reverse_rows, nodes, w_in, w_res, w_node):
    msg, tgt, rev, node = messages[0, 0], targets[0], reverse_rows[0, 0], nodes[0]
    edges, feat = msg.shape
    share = node.shape[0]
    points = share * rows_n
    layers = w_in.shape[0]
    blocks = len(OFFSETS)
    block = edges // blocks
    dma = pltpu.SemaphoreType.DMA
    vmem = pl.BlockSpec(memory_space=pltpu.VMEM)
    hbm = pl.BlockSpec(memory_space=pl.ANY)
    edge_out, node_out = pl.pallas_call(
        functools.partial(kernel, rows_n, cols_n),
        out_shape=(
            jax.ShapeDtypeStruct((edges, feat), BF16),
            jax.ShapeDtypeStruct((share, feat), BF16),
        ),
        in_specs=[vmem] * 4 + [hbm] * 3,
        out_specs=(hbm, hbm),
        scratch_shapes=[
            pltpu.VMEM(w_in.shape, BF16),
            pltpu.VMEM(w_res.shape, BF16),
            pltpu.VMEM(w_node.shape, BF16),
            pltpu.VMEM((edges, feat), BF16),
            pltpu.VMEM((edges, points), BF16),
            pltpu.VMEM((blocks, block, block), BF16),
            pltpu.VMEM((edges, feat), F32),
            pltpu.VMEM((share, feat), F32),
            pltpu.VMEM((edges, feat), BF16),
            pltpu.VMEM((edges, feat), F32),
            pltpu.VMEM((share, feat), BF16),
            pltpu.VMEM((layers, points, feat), BF16),
            pltpu.VMEM((layers, rows_n - 1, share, feat), BF16),
            pltpu.VMEM((layers, rows_n - 1, share, feat), BF16),
            pltpu.VMEM((layers, blocks, block, feat), BF16),
            pltpu.VMEM((layers, blocks - 2, block, feat), BF16),
            dma((layers, 3)),
            dma((layers, rows_n - 1)),
            dma((layers, rows_n - 1)),
            dma((layers, rows_n - 1)),
            dma((layers, rows_n - 1)),
            dma((layers, blocks - 2)),
            dma((layers, blocks - 2)),
            dma((blocks // 2 + 1,)),
        ],
        compiler_params=pltpu.CompilerParams(
            collective_id=0, has_side_effects=True, vmem_limit_bytes=56 * 2**20
        ),
        cost_estimate=pl.CostEstimate(
            flops=11 * 10**9, bytes_accessed=12 * 10**6, transcendentals=5 * 10**6
        ),
    )(msg, tgt, rev, node, w_in, w_res, w_node)
    return edge_out[None, None], node_out[None]


def solution(mesh):
    in_specs = (
        P("row", "col", None, None),
        P("row", "col", None),
        P("row", "col", None, None),
        P("col", "row", None),
        P(),
        P(),
        P(),
    )
    out_specs = (P("row", "col", None, None), P("col", "row", None))
    body = functools.partial(shards, mesh.shape["row"], mesh.shape["col"])
    return jax.shard_map(body, mesh=mesh, in_specs=in_specs, out_specs=out_specs, check_vma=False)
```

```python
import functools
import math

import jax
import jax.numpy as jnp
from jax import lax
from jax.experimental import pallas as pl
from jax.experimental.pallas import tpu as pltpu
from jax.sharding import PartitionSpec as P

OFFSETS = (0, 0, 1, -1, 2, -2, 3, -3)
ROOT_HALF = 0.7071067811865476
PIECES = 4
ORDER = (0, 3, 2, 1)
MESH = pl.DeviceIdType.MESH
F32 = jnp.float32
BF16 = jnp.bfloat16


def silu(v):
    half = 0.5 * v
    return half + half * jnp.tanh(half)


def mm(a, b):
    return jnp.dot(a, b, preferred_element_type=F32)


def kernel(
    rows_n,
    cols_n,
    msg,
    tgt,
    rev,
    node,
    w_in_hbm,
    w_res_hbm,
    w_node_hbm,
    edge_out,
    node_out,
    w_in,
    w_res,
    w_node,
    cur,
    hot_part,
    acc,
    onehot,
    perm,
    base,
    pre,
    h_own,
    h_tgt,
    h_all,
    part_out,
    part_in,
    u_out,
    u_in,
    w_sem,
    rs_send,
    rs_recv,
    ag_send,
    ag_recv,
    col_send,
    col_recv,
    out_sem,
):
    r, c = lax.axis_index("row"), lax.axis_index("col")
    edges, feat = msg.shape
    share = node.shape[0]
    points = share * rows_n
    blocks = len(OFFSETS)
    block = edges // blocks
    pair = 2 * block
    pairs = edges // pair
    half = points // 2
    agg_scale = 1.0 / math.sqrt(edges // share)
    layers = w_in_hbm.shape[0]
    along_x = rows_n // 2
    r_y, r_x = r // along_x, lax.rem(r, along_x)
    steps = [(dx, dy) for dy in (1, 0) for dx in (2, 1, 3, 0)]
    others = rows_n - 1

    def row_peer(j, sign=1):
        dx, dy = steps[j]
        x = lax.rem(r_x + along_x + sign * dx, along_x)
        return lax.rem(r_y + dy, 2) * along_x + x

    def col_peer(offset):
        return lax.rem(c + offset + cols_n, cols_n)

    def rows_of(device):
        return pl.ds(pl.multiple_of(device * share, share), share)

    barrier = pltpu.get_barrier_semaphore()
    for j in range(others):
        pl.semaphore_signal(barrier, inc=1, device_id=(row_peer(j), c), device_id_type=MESH)
    for off in OFFSETS[2:]:
        pl.semaphore_signal(barrier, inc=1, device_id=(r, col_peer(off)), device_id_type=MESH)

    loads = []
    for t in range(layers):
        for i, (src, dst) in enumerate(
            ((w_in_hbm, w_in), (w_node_hbm, w_node), (w_res_hbm, w_res))
        ):
            loads.append(pltpu.make_async_copy(src.at[t], dst.at[t], w_sem.at[t, i]))
            loads[-1].start()

    def rs_copy(t, j):
        return pltpu.make_async_remote_copy(
            src_ref=part_out.at[t, j],
            dst_ref=part_in.at[t, j],
            send_sem=rs_send.at[t, j],
            recv_sem=rs_recv.at[t, j],
            device_id=(row_peer(j), c),
            device_id_type=MESH,
        )

    def ag_copy(t, j):
        target = h_all.at[t, rows_of(r)]
        return pltpu.make_async_remote_copy(
            src_ref=target,
            dst_ref=target,
            send_sem=ag_send.at[t, j],
            recv_sem=ag_recv.at[t, j],
            device_id=(row_peer(j), c),
            device_id_type=MESH,
        )

    def ag_arrival(t, j):
        target = h_all.at[t, rows_of(row_peer(j, -1))]
        return pltpu.make_async_remote_copy(
            src_ref=target,
            dst_ref=target,
            send_sem=ag_send.at[t, j],
            recv_sem=ag_recv.at[t, j],
            device_id=(row_peer(j), c),
            device_id_type=MESH,
        )

    def col_copy(t, b):
        return pltpu.make_async_remote_copy(
            src_ref=u_out.at[t, b],
            dst_ref=u_in.at[t, (b ^ 1) - 2],
            send_sem=col_send.at[t, b - 2],
            recv_sem=col_recv.at[t, (b ^ 1) - 2],
            device_id=(r, col_peer(OFFSETS[b])),
            device_id_type=MESH,
        )

    def col_arrival(t, k):
        return pltpu.make_async_remote_copy(
            src_ref=u_out.at[t, k],
            dst_ref=u_in.at[t, k - 2],
            send_sem=col_send.at[t, k - 2],
            recv_sem=col_recv.at[t, k - 2],
            device_id=(r, col_peer(OFFSETS[k])),
            device_id_type=MESH,
        )

    def send_sums(t, part, sums):
        for i in range(rows_n // 2):
            j = part * (rows_n // 2) + i
            if j == others:
                continue
            part_out[t, j] = sums[i * share : (i + 1) * share].astype(BF16)
            if t == 0 and j == 0:
                pl.semaphore_wait(barrier, others + blocks - 2)
            rs_copy(t, j).start()

    for part in range(2):
        for i in range(rows_n // 2):
            j = part * (rows_n // 2) + i
            ids = lax.broadcasted_iota(jnp.int32, (share, edges), 0) + row_peer(j) * share
            hot_part[j * share : (j + 1) * share] = jnp.where(
                tgt[...] == ids, 1.0, 0.0
            ).astype(BF16)
        rows = pl.ds(part * half, half)
        sums = mm(hot_part[rows], msg[...])
        send_sums(0, part, sums)
        if part:
            acc[rows] = sums

    lane = lax.broadcasted_iota(jnp.int32, (block, block), 1)
    for k in range(blocks):
        rows = pl.ds(k * block, block)
        ids = jnp.broadcast_to(tgt[0:1, k * block : (k + 1) * block], (block, block)).T
        for i in range(points // block):
            onehot[rows, i * block : (i + 1) * block] = jnp.where(
                ids == lane + i * block, 1.0, 0.0
            ).astype(BF16)
        ids = jnp.broadcast_to(rev[k : k + 1, :], (block, block)).T
        perm[k] = jnp.where(ids == lane, 1.0, 0.0).astype(BF16)

    h_own[...] = node[...]
    for t in range(layers):
        last = t == layers - 1
        held = msg if t == 0 else cur
        loads[3 * t].wait()
        for q in range(pairs):
            rows = pl.ds(q * pair, pair)
            base[rows] = mm(held[rows], w_in[t, :feat])

        loads[3 * t + 1].wait()
        total = acc[others * share :]
        for j in range(others):
            rs_copy(t, j).wait_recv()
            total = total + part_in[t, j].astype(F32)
        scaled = (total * agg_scale).astype(BF16)
        h_new = (h_own[...].astype(F32) + silu(mm(scaled, w_node[t]))).astype(BF16)
        h_own[...] = h_new
        h_all[t, rows_of(r)] = h_new
        for j in range(others):
            ag_copy(t, j).start()
        if last:
            node_copy = pltpu.make_async_copy(h_own, node_out, out_sem.at[pairs])
            node_copy.start()
        for j in range(others):
            ag_arrival(t, j).wait_recv()

        for q in (3, 2, 1, 0):
            rows = pl.ds(q * pair, pair)
            picked = mm(onehot[rows], h_all[t]).astype(BF16)
            h_tgt[rows] = picked
            u = (base[rows] + mm(picked, w_in[t, feat : 2 * feat])).astype(BF16)
            for i in range(2):
                b = 2 * q + i
                u_out[t, b] = u[i * block : (i + 1) * block]
                if q:
                    col_copy(t, b).start()
        for q in ORDER:
            rows = pl.ds(q * pair, pair)
            pre[rows] = mm(h_tgt[rows], w_in[t, 2 * feat :])

        loads[3 * t + 2].wait()
        for q in ORDER:
            rows = pl.ds(q * pair, pair)
            moved = []
            for k in (2 * q, 2 * q + 1):
                if q:
                    col_arrival(t, k).wait_recv()
                    moved.append(mm(perm[k], u_in[t, k - 2]))
                else:
                    moved.append(mm(perm[k], u_out[t, k ^ 1]))
            hidden = silu(pre[rows] + jnp.concatenate(moved, axis=0)).astype(BF16)
            inner = silu(mm(hidden, w_res[t, 0, 0])).astype(BF16)
            hidden = (
                (hidden.astype(F32) + silu(mm(inner, w_res[t, 0, 1]))) * ROOT_HALF
            ).astype(BF16)
            inner = silu(mm(hidden, w_res[t, 1, 0])).astype(BF16)
            summed = (hidden.astype(F32) + silu(mm(inner, w_res[t, 1, 1]))) * ROOT_HALF
            new = ((held[rows].astype(F32) + summed) * ROOT_HALF).astype(BF16)
            cur[rows] = new
            if last:
                pltpu.make_async_copy(cur.at[rows], edge_out.at[rows], out_sem.at[q]).start()
                continue
            columns = slice(q * pair, (q + 1) * pair)
            for part in range(2):
                points_of = pl.ds(part * half, half)
                sums = mm(hot_part[points_of, columns], new)
                if q:
                    sums = acc[points_of] + sums
                if q == ORDER[-1]:
                    send_sums(t + 1, part, sums)
                if q != ORDER[-1] or part:
                    acc[points_of] = sums

    for t in range(layers):
        for j in range(others):
            rs_copy(t, j).wait_send()
            ag_copy(t, j).wait_send()
        for b in range(2, blocks):
            col_copy(t, b).wait_send()
    for q in range(pairs):
        rows = pl.ds(q * pair, pair)
        pltpu.make_async_copy(cur.at[rows], edge_out.at[rows], out_sem.at[q]).wait()
    node_copy.wait()


def hand_over(edge_in, node_in, edge_out, node_out, edge_held, node_held, sems):
    piece = edge_in.shape[0] // PIECES
    moves = [(node_in, node_held, node_out)]
    for i in range(PIECES):
        rows = pl.ds(i * piece, piece)
        moves.append((edge_in.at[rows], edge_held.at[rows], edge_out.at[rows]))
    loads = [pltpu.make_async_copy(m[0], m[1], sems.at[0, i]) for i, m in enumerate(moves)]
    stores = [pltpu.make_async_copy(m[1], m[2], sems.at[1, i]) for i, m in enumerate(moves)]
    for copy in loads:
        copy.start()
    for load, store in zip(loads, stores):
        load.wait()
        store.start()
    for copy in stores:
        copy.wait()


def shards(rows_n, cols_n, messages, targets, reverse_rows, nodes, w_in, w_res, w_node):
    msg, tgt, rev, node = messages[0, 0], targets[0], reverse_rows[0, 0], nodes[0]
    edges, feat = msg.shape
    share = node.shape[0]
    points = share * rows_n
    layers = w_in.shape[0]
    blocks = len(OFFSETS)
    block = edges // blocks
    dma = pltpu.SemaphoreType.DMA
    vmem = pl.BlockSpec(memory_space=pltpu.VMEM)
    hbm = pl.BlockSpec(memory_space=pl.ANY)
    shapes = (
        jax.ShapeDtypeStruct((edges, feat), BF16),
        jax.ShapeDtypeStruct((share, feat), BF16),
    )
    held = pl.pallas_call(
        functools.partial(kernel, rows_n, cols_n),
        out_shape=shapes,
        in_specs=[vmem] * 4 + [hbm] * 3,
        out_specs=(hbm, hbm),
        scratch_shapes=[
            pltpu.VMEM(w_in.shape, BF16),
            pltpu.VMEM(w_res.shape, BF16),
            pltpu.VMEM(w_node.shape, BF16),
            pltpu.VMEM((edges, feat), BF16),
            pltpu.VMEM((points, edges), BF16),
            pltpu.VMEM((points, feat), F32),
            pltpu.VMEM((edges, points), BF16),
            pltpu.VMEM((blocks, block, block), BF16),
            pltpu.VMEM((edges, feat), F32),
            pltpu.VMEM((edges, feat), F32),
            pltpu.VMEM((share, feat), BF16),
            pltpu.VMEM((edges, feat), BF16),
            pltpu.VMEM((layers, points, feat), BF16),
            pltpu.VMEM((layers, rows_n - 1, share, feat), BF16),
            pltpu.VMEM((layers, rows_n - 1, share, feat), BF16),
            pltpu.VMEM((layers, blocks, block, feat), BF16),
            pltpu.VMEM((layers, blocks - 2, block, feat), BF16),
            dma((layers, 3)),
            dma((layers, rows_n - 1)),
            dma((layers, rows_n - 1)),
            dma((layers, rows_n - 1)),
            dma((layers, rows_n - 1)),
            dma((layers, blocks - 2)),
            dma((layers, blocks - 2)),
            dma((blocks // 2 + 1,)),
        ],
        compiler_params=pltpu.CompilerParams(
            collective_id=0, has_side_effects=True, vmem_limit_bytes=56 * 2**20
        ),
        cost_estimate=pl.CostEstimate(
            flops=11 * 10**9, bytes_accessed=12 * 10**6, transcendentals=5 * 10**6
        ),
    )(msg, tgt, rev, node, w_in, w_res, w_node)
    edge_out, node_out = pl.pallas_call(
        hand_over,
        out_shape=shapes,
        in_specs=[hbm] * 2,
        out_specs=(hbm, hbm),
        scratch_shapes=[pltpu.VMEM((edges, feat), BF16), pltpu.VMEM((share, feat), BF16), dma((2, PIECES + 1))],
    )(*held)
    return edge_out[None, None], node_out[None]


def solution(mesh):
    in_specs = (
        P("row", "col", None, None),
        P("row", "col", None),
        P("row", "col", None, None),
        P("col", "row", None),
        P(),
        P(),
        P(),
    )
    out_specs = (P("row", "col", None, None), P("col", "row", None))
    body = functools.partial(shards, mesh.shape["row"], mesh.shape["col"])
    return jax.shard_map(body, mesh=mesh, in_specs=in_specs, out_specs=out_specs, check_vma=False)
```

```python
import functools
import math

import jax
import jax.numpy as jnp
from jax import lax
from jax.experimental import pallas as pl
from jax.experimental.pallas import tpu as pltpu
from jax.sharding import PartitionSpec as P

OFFSETS = (0, 0, 1, -1, 2, -2, 3, -3)
ROOT_HALF = 0.7071067811865476
PARTS = 2
PIECES = 4
ORDER = (0, 3, 2, 1)
MESH = pl.DeviceIdType.MESH
F32 = jnp.float32
BF16 = jnp.bfloat16


def silu(v):
    half = 0.5 * v
    return half + half * jnp.tanh(half)


def mm(a, b):
    return jnp.dot(a, b, preferred_element_type=F32)


def kernel(
    rows_n,
    cols_n,
    msg_hbm,
    tgt_hbm,
    rev_hbm,
    node_hbm,
    w_in_hbm,
    w_res_hbm,
    w_node_hbm,
    edge_out,
    node_out,
    w_in,
    w_res,
    w_node,
    tgt,
    rev,
    msg,
    cur,
    hot_part,
    acc,
    onehot,
    perm,
    base,
    pre,
    h_own,
    h_tgt,
    h_all,
    part_out,
    part_in,
    u_out,
    u_in,
    w_sem,
    rs_send,
    rs_recv,
    ag_send,
    ag_recv,
    col_send,
    col_recv,
    in_sem,
    out_sem,
):
    r, c = lax.axis_index("row"), lax.axis_index("col")
    edges, feat = msg_hbm.shape
    share = node_hbm.shape[0]
    points = share * rows_n
    blocks = len(OFFSETS)
    block = edges // blocks
    pair = 2 * block
    pairs = edges // pair
    group = points // PARTS
    piece = share // PARTS
    agg_scale = 1.0 / math.sqrt(edges // share)
    layers = w_in_hbm.shape[0]
    along_x = rows_n // 2
    r_y, r_x = r // along_x, lax.rem(r, along_x)
    steps = [(dx, dy) for dy in (1, 0) for dx in (2, 1, 3, 0)]
    others = rows_n - 1

    def row_peer(j, sign=1):
        dx, dy = steps[j]
        x = lax.rem(r_x + along_x + sign * dx, along_x)
        return lax.rem(r_y + dy, 2) * along_x + x

    def col_peer(offset):
        return lax.rem(c + offset + cols_n, cols_n)

    def rows_of(device, part):
        return pl.ds(pl.multiple_of(device * share + part * piece, piece), piece)

    barrier = pltpu.get_barrier_semaphore()
    for j in range(others):
        pl.semaphore_signal(barrier, inc=1, device_id=(row_peer(j), c), device_id_type=MESH)
    for off in OFFSETS[2:]:
        pl.semaphore_signal(barrier, inc=1, device_id=(r, col_peer(off)), device_id_type=MESH)

    firsts = []
    for i, (src, dst) in enumerate(
        ((tgt_hbm, tgt), (msg_hbm, msg), (rev_hbm, rev), (node_hbm, h_own))
    ):
        firsts.append(pltpu.make_async_copy(src, dst, in_sem.at[i]))
        firsts[-1].start()
    loads = []
    for t in range(layers):
        for i, (src, dst) in enumerate(
            ((w_in_hbm, w_in), (w_node_hbm, w_node), (w_res_hbm, w_res))
        ):
            loads.append(pltpu.make_async_copy(src.at[t], dst.at[t], w_sem.at[t, i]))
            loads[-1].start()

    def rs_copy(t, part, j):
        return pltpu.make_async_remote_copy(
            src_ref=part_out.at[t, part, j],
            dst_ref=part_in.at[t, part, j],
            send_sem=rs_send.at[t, part, j],
            recv_sem=rs_recv.at[t, part, j],
            device_id=(row_peer(j), c),
            device_id_type=MESH,
        )

    def ag_copy(t, part, j):
        target = h_all.at[t, rows_of(r, part)]
        return pltpu.make_async_remote_copy(
            src_ref=target,
            dst_ref=target,
            send_sem=ag_send.at[t, part, j],
            recv_sem=ag_recv.at[t, part, j],
            device_id=(row_peer(j), c),
            device_id_type=MESH,
        )

    def ag_arrival(t, part, j):
        target = h_all.at[t, rows_of(row_peer(j, -1), part)]
        return pltpu.make_async_remote_copy(
            src_ref=target,
            dst_ref=target,
            send_sem=ag_send.at[t, part, j],
            recv_sem=ag_recv.at[t, part, j],
            device_id=(row_peer(j), c),
            device_id_type=MESH,
        )

    def col_copy(t, b):
        return pltpu.make_async_remote_copy(
            src_ref=u_out.at[t, b],
            dst_ref=u_in.at[t, (b ^ 1) - 2],
            send_sem=col_send.at[t, b - 2],
            recv_sem=col_recv.at[t, (b ^ 1) - 2],
            device_id=(r, col_peer(OFFSETS[b])),
            device_id_type=MESH,
        )

    def col_arrival(t, k):
        return pltpu.make_async_remote_copy(
            src_ref=u_out.at[t, k],
            dst_ref=u_in.at[t, k - 2],
            send_sem=col_send.at[t, k - 2],
            recv_sem=col_recv.at[t, k - 2],
            device_id=(r, col_peer(OFFSETS[k])),
            device_id_type=MESH,
        )

    def send_sums(t, part, sums):
        for j in range(others):
            part_out[t, part, j] = sums[j * piece : (j + 1) * piece].astype(BF16)
            if t == 0 and part == 0 and j == 0:
                pl.semaphore_wait(barrier, others + blocks - 2)
            rs_copy(t, part, j).start()
        acc[part * group + others * piece : (part + 1) * group] = sums[others * piece :]

    firsts[0].wait()
    for part in range(PARTS):
        for j in range(rows_n):
            ids = lax.broadcasted_iota(jnp.int32, (piece, edges), 0) + (
                row_peer(j) * share + part * piece
            )
            first = part * group + j * piece
            hot_part[first : first + piece] = jnp.where(tgt[...] == ids, 1.0, 0.0).astype(BF16)
        if part == 0:
            firsts[1].wait()
        send_sums(0, part, mm(hot_part[part * group : (part + 1) * group], msg[...]))

    firsts[2].wait()
    lane = lax.broadcasted_iota(jnp.int32, (block, block), 1)
    for k in range(blocks):
        rows = pl.ds(k * block, block)
        ids = jnp.broadcast_to(tgt[0:1, k * block : (k + 1) * block], (block, block)).T
        for i in range(points // block):
            onehot[rows, i * block : (i + 1) * block] = jnp.where(
                ids == lane + i * block, 1.0, 0.0
            ).astype(BF16)
        ids = jnp.broadcast_to(rev[k : k + 1, :], (block, block)).T
        perm[k] = jnp.where(ids == lane, 1.0, 0.0).astype(BF16)

    firsts[3].wait()
    edge_copies = []
    for t in range(layers):
        last = t == layers - 1
        held = msg if t == 0 else cur
        loads[3 * t].wait()
        for q in range(pairs):
            rows = pl.ds(q * pair, pair)
            base[rows] = mm(held[rows], w_in[t, :feat])

        loads[3 * t + 1].wait()
        for part in range(PARTS):
            total = acc[part * group + others * piece : (part + 1) * group]
            for j in range(others):
                rs_copy(t, part, j).wait_recv()
                total = total + part_in[t, part, j].astype(F32)
            scaled = (total * agg_scale).astype(BF16)
            mine = slice(part * piece, (part + 1) * piece)
            h_new = (h_own[mine].astype(F32) + silu(mm(scaled, w_node[t]))).astype(BF16)
            h_own[mine] = h_new
            h_all[t, rows_of(r, part)] = h_new
            for j in range(others):
                ag_copy(t, part, j).start()
        if last:
            node_copy = pltpu.make_async_copy(h_own, node_out, out_sem.at[pairs])
            node_copy.start()
        for part in range(PARTS):
            for j in range(others):
                ag_arrival(t, part, j).wait_recv()

        for q in (3, 2, 1, 0):
            rows = pl.ds(q * pair, pair)
            picked = mm(onehot[rows], h_all[t]).astype(BF16)
            h_tgt[rows] = picked
            u = (base[rows] + mm(picked, w_in[t, feat : 2 * feat])).astype(BF16)
            for i in range(2):
                b = 2 * q + i
                u_out[t, b] = u[i * block : (i + 1) * block]
                if q:
                    col_copy(t, b).start()
        for q in ORDER:
            rows = pl.ds(q * pair, pair)
            pre[rows] = mm(h_tgt[rows], w_in[t, 2 * feat :])

        loads[3 * t + 2].wait()
        for q in ORDER:
            rows = pl.ds(q * pair, pair)
            moved = []
            for k in (2 * q, 2 * q + 1):
                if q:
                    col_arrival(t, k).wait_recv()
                    moved.append(mm(perm[k], u_in[t, k - 2]))
                else:
                    moved.append(mm(perm[k], u_out[t, k ^ 1]))
            hidden = silu(pre[rows] + jnp.concatenate(moved, axis=0)).astype(BF16)
            inner = silu(mm(hidden, w_res[t, 0, 0])).astype(BF16)
            hidden = (
                (hidden.astype(F32) + silu(mm(inner, w_res[t, 0, 1]))) * ROOT_HALF
            ).astype(BF16)
            inner = silu(mm(hidden, w_res[t, 1, 0])).astype(BF16)
            summed = (hidden.astype(F32) + silu(mm(inner, w_res[t, 1, 1]))) * ROOT_HALF
            new = ((held[rows].astype(F32) + summed) * ROOT_HALF).astype(BF16)
            cur[rows] = new
            if last:
                edge_copies.append(pltpu.make_async_copy(cur.at[rows], edge_out.at[rows], out_sem.at[q]))
                edge_copies[-1].start()
                continue
            columns = slice(q * pair, (q + 1) * pair)
            for part in range(PARTS):
                points_of = pl.ds(part * group, group)
                sums = mm(hot_part[points_of, columns], new)
                if q != ORDER[0]:
                    sums = acc[points_of] + sums
                if q == ORDER[-1]:
                    send_sums(t + 1, part, sums)
                else:
                    acc[points_of] = sums

    for t in range(layers):
        for part in range(PARTS):
            for j in range(others):
                rs_copy(t, part, j).wait_send()
                ag_copy(t, part, j).wait_send()
        for b in range(2, blocks):
            col_copy(t, b).wait_send()
    for copy in edge_copies:
        copy.wait()
    node_copy.wait()


def hand_over(edge_in, node_in, edge_out, node_out, edge_held, node_held, sems):
    piece = edge_in.shape[0] // PIECES
    moves = [(node_in, node_held, node_out)]
    for i in range(PIECES):
        rows = pl.ds(i * piece, piece)
        moves.append((edge_in.at[rows], edge_held.at[rows], edge_out.at[rows]))
    loads = [pltpu.make_async_copy(m[0], m[1], sems.at[0, i]) for i, m in enumerate(moves)]
    stores = [pltpu.make_async_copy(m[1], m[2], sems.at[1, i]) for i, m in enumerate(moves)]
    for copy in loads:
        copy.start()
    for load, store in zip(loads, stores):
        load.wait()
        store.start()
    for copy in stores:
        copy.wait()


def shards(rows_n, cols_n, messages, targets, reverse_rows, nodes, w_in, w_res, w_node):
    msg, tgt, rev, node = messages[0, 0], targets[0], reverse_rows[0, 0], nodes[0]
    edges, feat = msg.shape
    share = node.shape[0]
    points = share * rows_n
    layers = w_in.shape[0]
    blocks = len(OFFSETS)
    block = edges // blocks
    dma = pltpu.SemaphoreType.DMA
    hbm = pl.BlockSpec(memory_space=pltpu.HBM)
    shapes = (
        jax.ShapeDtypeStruct((edges, feat), BF16),
        jax.ShapeDtypeStruct((share, feat), BF16),
    )
    held = pl.pallas_call(
        functools.partial(kernel, rows_n, cols_n),
        out_shape=shapes,
        in_specs=[hbm] * 7,
        out_specs=(hbm, hbm),
        scratch_shapes=[
            pltpu.VMEM(w_in.shape, BF16),
            pltpu.VMEM(w_res.shape, BF16),
            pltpu.VMEM(w_node.shape, BF16),
            pltpu.VMEM(tgt.shape, tgt.dtype),
            pltpu.VMEM(rev.shape, rev.dtype),
            pltpu.VMEM((edges, feat), BF16),
            pltpu.VMEM((edges, feat), BF16),
            pltpu.VMEM((points, edges), BF16),
            pltpu.VMEM((points, feat), F32),
            pltpu.VMEM((edges, points), BF16),
            pltpu.VMEM((blocks, block, block), BF16),
            pltpu.VMEM((edges, feat), F32),
            pltpu.VMEM((edges, feat), F32),
            pltpu.VMEM((share, feat), BF16),
            pltpu.VMEM((edges, feat), BF16),
            pltpu.VMEM((layers, points, feat), BF16),
            pltpu.VMEM((layers, PARTS, rows_n - 1, share // PARTS, feat), BF16),
            pltpu.VMEM((layers, PARTS, rows_n - 1, share // PARTS, feat), BF16),
            pltpu.VMEM((layers, blocks, block, feat), BF16),
            pltpu.VMEM((layers, blocks - 2, block, feat), BF16),
            dma((layers, 3)),
            dma((layers, PARTS, rows_n - 1)),
            dma((layers, PARTS, rows_n - 1)),
            dma((layers, PARTS, rows_n - 1)),
            dma((layers, PARTS, rows_n - 1)),
            dma((layers, blocks - 2)),
            dma((layers, blocks - 2)),
            dma((4,)),
            dma((blocks // 2 + 1,)),
        ],
        compiler_params=pltpu.CompilerParams(
            collective_id=0, has_side_effects=True, vmem_limit_bytes=56 * 2**20
        ),
        cost_estimate=pl.CostEstimate(
            flops=11 * 10**9, bytes_accessed=12 * 10**6, transcendentals=5 * 10**6
        ),
    )(msg, tgt, rev, node, w_in, w_res, w_node)
    edge_out, node_out = pl.pallas_call(
        hand_over,
        out_shape=shapes,
        in_specs=[hbm] * 2,
        out_specs=(hbm, hbm),
        scratch_shapes=[pltpu.VMEM((edges, feat), BF16), pltpu.VMEM((share, feat), BF16), dma((2, PIECES + 1))],
    )(*held)
    return edge_out[None, None], node_out[None]


def solution(mesh):
    in_specs = (
        P("row", "col", None, None),
        P("row", "col", None),
        P("row", "col", None, None),
        P("col", "row", None),
        P(),
        P(),
        P(),
    )
    out_specs = (P("row", "col", None, None), P("col", "row", None))
    body = functools.partial(shards, mesh.shape["row"], mesh.shape["col"])
    return jax.shard_map(body, mesh=mesh, in_specs=in_specs, out_specs=out_specs, check_vma=False)
```

```python
import functools
import math

import jax
import jax.numpy as jnp
from jax import lax
from jax.experimental import pallas as pl
from jax.experimental.pallas import tpu as pltpu
from jax.sharding import PartitionSpec as P

OFFSETS = (0, 0, 1, -1, 2, -2, 3, -3)
ROOT_HALF = 0.7071067811865476
PARTS = 2
PIECES = 4
ORDER = (0, 3, 2, 1)
MESH = pl.DeviceIdType.MESH
F32 = jnp.float32
BF16 = jnp.bfloat16


def silu(v):
    half = 0.5 * v
    return half + half * jnp.tanh(half)


def mm(a, b):
    return jnp.dot(a, b, preferred_element_type=F32)


def kernel(
    rows_n,
    cols_n,
    msg_hbm,
    tgt_hbm,
    rev_hbm,
    node_hbm,
    w_in_hbm,
    w_res_hbm,
    w_node_hbm,
    edge_out,
    node_out,
    w_in,
    w_res,
    w_node,
    tgt,
    rev,
    msg,
    cur,
    hot_part,
    acc,
    onehot,
    onehot_sent,
    perm,
    m_sent,
    base,
    pre,
    h_own,
    h_all,
    part_out,
    part_in,
    u_out,
    u_in,
    w_sem,
    rs_send,
    rs_recv,
    ag_send,
    ag_recv,
    col_send,
    col_recv,
    in_sem,
    out_sem,
):
    r, c = lax.axis_index("row"), lax.axis_index("col")
    edges, feat = msg_hbm.shape
    share = node_hbm.shape[0]
    points = share * rows_n
    blocks = len(OFFSETS)
    block = edges // blocks
    pair = 2 * block
    pairs = edges // pair
    group = points // PARTS
    piece = share // PARTS
    agg_scale = 1.0 / math.sqrt(edges // share)
    layers = w_in_hbm.shape[0]
    along_x = rows_n // 2
    r_y, r_x = r // along_x, lax.rem(r, along_x)
    steps = [(dx, dy) for dy in (1, 0) for dx in (2, 1, 3, 0)]
    others = rows_n - 1

    def row_peer(j, sign=1):
        dx, dy = steps[j]
        x = lax.rem(r_x + along_x + sign * dx, along_x)
        return lax.rem(r_y + dy, 2) * along_x + x

    def col_peer(offset):
        return lax.rem(c + offset + cols_n, cols_n)

    def rows_of(device, part):
        return pl.ds(pl.multiple_of(device * share + part * piece, piece), piece)

    barrier = pltpu.get_barrier_semaphore()
    for j in range(others):
        pl.semaphore_signal(barrier, inc=1, device_id=(row_peer(j), c), device_id_type=MESH)
    for off in OFFSETS[2:]:
        pl.semaphore_signal(barrier, inc=1, device_id=(r, col_peer(off)), device_id_type=MESH)

    firsts = []
    for i, (src, dst) in enumerate(
        ((tgt_hbm, tgt), (msg_hbm, msg), (rev_hbm, rev), (node_hbm, h_own))
    ):
        firsts.append(pltpu.make_async_copy(src, dst, in_sem.at[i]))
        firsts[-1].start()
    def rs_copy(t, part, j):
        return pltpu.make_async_remote_copy(
            src_ref=part_out.at[t, part, j],
            dst_ref=part_in.at[t, part, j],
            send_sem=rs_send.at[t, part],
            recv_sem=rs_recv.at[t, part],
            device_id=(row_peer(j), c),
            device_id_type=MESH,
        )

    def ag_copy(t, part, j):
        target = h_all.at[t, rows_of(r, part)]
        return pltpu.make_async_remote_copy(
            src_ref=target,
            dst_ref=target,
            send_sem=ag_send.at[t, part],
            recv_sem=ag_recv.at[t, part],
            device_id=(row_peer(j), c),
            device_id_type=MESH,
        )

    def rs_all(t, part):
        return pltpu.make_async_remote_copy(
            src_ref=part_out.at[t, part],
            dst_ref=part_in.at[t, part],
            send_sem=rs_send.at[t, part],
            recv_sem=rs_recv.at[t, part],
            device_id=(row_peer(0), c),
            device_id_type=MESH,
        )

    def ag_all(t, part):
        rows = h_all.at[t, pl.ds(0, others * piece)]
        return pltpu.make_async_remote_copy(
            src_ref=rows,
            dst_ref=rows,
            send_sem=ag_send.at[t, part],
            recv_sem=ag_recv.at[t, part],
            device_id=(row_peer(0), c),
            device_id_type=MESH,
        )

    def blocks_of(q):
        return (2 * q, 2 * q + 1) if q else ()

    def col_copy(t, b):
        return pltpu.make_async_remote_copy(
            src_ref=u_out.at[t, b],
            dst_ref=u_in.at[t, (b ^ 1) - 2],
            send_sem=col_send.at[t, b - 2],
            recv_sem=col_recv.at[t, (b ^ 1) - 2],
            device_id=(r, col_peer(OFFSETS[b])),
            device_id_type=MESH,
        )

    def col_arrival(t, k):
        return pltpu.make_async_remote_copy(
            src_ref=u_out.at[t, k],
            dst_ref=u_in.at[t, k - 2],
            send_sem=col_send.at[t, k - 2],
            recv_sem=col_recv.at[t, k - 2],
            device_id=(r, col_peer(OFFSETS[k])),
            device_id_type=MESH,
        )

    def send_sums(t, part, sums):
        for j in range(others):
            part_out[t, part, j] = sums[j * piece : (j + 1) * piece].astype(BF16)
            if t == 0 and part == 0 and j == 0:
                pl.semaphore_wait(barrier, others + blocks - 2)
            rs_copy(t, part, j).start()
        acc[part * group + others * piece : (part + 1) * group] = sums[others * piece :]

    firsts[0].wait()
    for part in range(PARTS):
        for j in range(rows_n):
            ids = lax.broadcasted_iota(jnp.int32, (piece, edges), 0) + (
                row_peer(j) * share + part * piece
            )
            first = part * group + j * piece
            hot_part[first : first + piece] = jnp.where(tgt[...] == ids, 1.0, 0.0).astype(BF16)
        if part == 0:
            firsts[1].wait()
        send_sums(0, part, mm(hot_part[part * group : (part + 1) * group], msg[...]))

    loads = []
    for t in range(layers):
        for i, (src, dst) in enumerate(
            ((w_in_hbm, w_in), (w_node_hbm, w_node), (w_res_hbm, w_res))
        ):
            loads.append(pltpu.make_async_copy(src.at[t], dst.at[t], w_sem.at[t, i]))
            loads[-1].start()

    firsts[2].wait()
    lane = lax.broadcasted_iota(jnp.int32, (block, block), 1)
    sublane = lax.broadcasted_iota(jnp.int32, (block, block), 0)
    for k in range(blocks):
        rows = pl.ds(k * block, block)
        ids = jnp.broadcast_to(tgt[0:1, k * block : (k + 1) * block], (block, block)).T
        for i in range(points // block):
            onehot[rows, i * block : (i + 1) * block] = jnp.where(
                ids == lane + i * block, 1.0, 0.0
            ).astype(BF16)
        ids = jnp.broadcast_to(rev[k : k + 1, :], (block, block))
        perm[k] = jnp.where(ids == sublane, 1.0, 0.0).astype(BF16)
        onehot_sent[rows] = mm(perm[k], onehot[rows]).astype(BF16)

    firsts[3].wait()
    edge_copies = []
    for t in range(layers):
        last = t == layers - 1
        held = msg if t == 0 else cur
        loads[3 * t].wait()
        for k in range(blocks):
            rows = pl.ds(k * block, block)
            m_sent[rows] = mm(perm[k], held[rows]).astype(BF16)
        for q in range(pairs):
            rows = pl.ds(q * pair, pair)
            base[rows] = mm(m_sent[rows], w_in[t, :feat])

        loads[3 * t + 1].wait()
        for part in range(PARTS):
            total = acc[part * group + others * piece : (part + 1) * group]
            rs_all(t, part).wait_recv()
            for j in range(others):
                total = total + part_in[t, part, j].astype(F32)
            scaled = (total * agg_scale).astype(BF16)
            mine = slice(part * piece, (part + 1) * piece)
            h_new = (h_own[mine].astype(F32) + silu(mm(scaled, w_node[t]))).astype(BF16)
            h_own[mine] = h_new
            h_all[t, rows_of(r, part)] = h_new
            for j in range(others):
                ag_copy(t, part, j).start()
        if last:
            node_copy = pltpu.make_async_copy(h_own, node_out, out_sem.at[pairs])
            node_copy.start()
        for part in range(PARTS):
            ag_all(t, part).wait_recv()

        for q in (3, 2, 1, 0):
            rows = pl.ds(q * pair, pair)
            picked = mm(onehot_sent[rows], h_all[t]).astype(BF16)
            u = (base[rows] + mm(picked, w_in[t, feat : 2 * feat])).astype(BF16)
            for i in range(2):
                u_out[t, 2 * q + i] = u[i * block : (i + 1) * block]
            for b in blocks_of(q):
                col_copy(t, b).start()
        for q in ORDER:
            rows = pl.ds(q * pair, pair)
            picked = mm(onehot[rows], h_all[t]).astype(BF16)
            pre[rows] = mm(picked, w_in[t, 2 * feat :])

        loads[3 * t + 2].wait()
        def edge_layer(x1, m):
            hidden = silu(x1).astype(BF16)
            inner = silu(mm(hidden, w_res[t, 0, 0])).astype(BF16)
            hidden = (
                (hidden.astype(F32) + silu(mm(inner, w_res[t, 0, 1]))) * ROOT_HALF
            ).astype(BF16)
            inner = silu(mm(hidden, w_res[t, 1, 0])).astype(BF16)
            summed = (hidden.astype(F32) + silu(mm(inner, w_res[t, 1, 1]))) * ROOT_HALF
            return ((m.astype(F32) + summed) * ROOT_HALF).astype(BF16)

        for part in range(PARTS):
            rs_all(t, part).wait_send()
            ag_all(t, part).wait_send()
        if t:
            for b in blocks_of(ORDER[-1]):
                col_copy(t - 1, b).wait_send()
        for n, q in enumerate(ORDER):
            if n > 1:
                for b in blocks_of(ORDER[n - 1]):
                    col_copy(t, b).wait_send()
            rows = pl.ds(q * pair, pair)
            arrived = []
            for k in (2 * q, 2 * q + 1):
                if q:
                    col_arrival(t, k).wait_recv()
                    arrived.append(u_in[t, k - 2])
                else:
                    arrived.append(u_out[t, k ^ 1])
            sums = pre[rows] + jnp.concatenate(arrived, axis=0).astype(F32)
            cur[rows] = edge_layer(sums, held[rows])
            if last:
                edge_copies.append(
                    pltpu.make_async_copy(cur.at[rows], edge_out.at[rows], out_sem.at[q])
                )
                edge_copies[-1].start()
            if last:
                continue
            columns = slice(q * pair, (q + 1) * pair)
            for part in range(PARTS):
                points_of = pl.ds(part * group, group)
                sums = mm(hot_part[points_of, columns], cur[rows])
                if q != ORDER[0]:
                    sums = acc[points_of] + sums
                if q == ORDER[-1]:
                    send_sums(t + 1, part, sums)
                else:
                    acc[points_of] = sums

    for b in blocks_of(ORDER[-1]):
        col_copy(layers - 1, b).wait_send()
    for copy in edge_copies:
        copy.wait()
    node_copy.wait()


def hand_over(edge_in, node_in, edge_out, node_out, edge_held, node_held, sems):
    piece = edge_in.shape[0] // PIECES
    moves = [(node_in, node_held, node_out)]
    for i in range(PIECES):
        rows = pl.ds(i * piece, piece)
        moves.append((edge_in.at[rows], edge_held.at[rows], edge_out.at[rows]))
    loads = [pltpu.make_async_copy(m[0], m[1], sems.at[0, i]) for i, m in enumerate(moves)]
    stores = [pltpu.make_async_copy(m[1], m[2], sems.at[1, i]) for i, m in enumerate(moves)]
    for copy in loads:
        copy.start()
    for load, store in zip(loads, stores):
        load.wait()
        store.start()
    for copy in stores:
        copy.wait()


def shards(rows_n, cols_n, messages, targets, reverse_rows, nodes, w_in, w_res, w_node):
    msg, tgt, rev, node = messages[0, 0], targets[0], reverse_rows[0, 0], nodes[0]
    edges, feat = msg.shape
    share = node.shape[0]
    points = share * rows_n
    layers = w_in.shape[0]
    blocks = len(OFFSETS)
    block = edges // blocks
    dma = pltpu.SemaphoreType.DMA
    hbm = pl.BlockSpec(memory_space=pltpu.HBM)
    shapes = (
        jax.ShapeDtypeStruct((edges, feat), BF16),
        jax.ShapeDtypeStruct((share, feat), BF16),
    )
    held = pl.pallas_call(
        functools.partial(kernel, rows_n, cols_n),
        out_shape=shapes,
        in_specs=[hbm] * 7,
        out_specs=(hbm, hbm),
        scratch_shapes=[
            pltpu.VMEM(w_in.shape, BF16),
            pltpu.VMEM(w_res.shape, BF16),
            pltpu.VMEM(w_node.shape, BF16),
            pltpu.VMEM(tgt.shape, tgt.dtype),
            pltpu.VMEM(rev.shape, rev.dtype),
            pltpu.VMEM((edges, feat), BF16),
            pltpu.VMEM((edges, feat), BF16),
            pltpu.VMEM((points, edges), BF16),
            pltpu.VMEM((points, feat), F32),
            pltpu.VMEM((edges, points), BF16),
            pltpu.VMEM((edges, points), BF16),
            pltpu.VMEM((blocks, block, block), BF16),
            pltpu.VMEM((edges, feat), BF16),
            pltpu.VMEM((edges, feat), F32),
            pltpu.VMEM((edges, feat), F32),
            pltpu.VMEM((share, feat), BF16),
            pltpu.VMEM((layers, points, feat), BF16),
            pltpu.VMEM((layers, PARTS, rows_n - 1, share // PARTS, feat), BF16),
            pltpu.VMEM((layers, PARTS, rows_n - 1, share // PARTS, feat), BF16),
            pltpu.VMEM((layers, blocks, block, feat), BF16),
            pltpu.VMEM((layers, blocks - 2, block, feat), BF16),
            dma((layers, 3)),
            dma((layers, PARTS)),
            dma((layers, PARTS)),
            dma((layers, PARTS)),
            dma((layers, PARTS)),
            dma((layers, blocks - 2)),
            dma((layers, blocks - 2)),
            dma((4,)),
            dma((blocks // 2 + 1,)),
        ],
        compiler_params=pltpu.CompilerParams(
            collective_id=0, has_side_effects=True, vmem_limit_bytes=56 * 2**20
        ),
        cost_estimate=pl.CostEstimate(
            flops=11 * 10**9, bytes_accessed=12 * 10**6, transcendentals=5 * 10**6
        ),
    )(msg, tgt, rev, node, w_in, w_res, w_node)
    edge_out, node_out = pl.pallas_call(
        hand_over,
        out_shape=shapes,
        in_specs=[hbm] * 2,
        out_specs=(hbm, hbm),
        scratch_shapes=[pltpu.VMEM((edges, feat), BF16), pltpu.VMEM((share, feat), BF16), dma((2, PIECES + 1))],
    )(*held)
    return edge_out[None, None], node_out[None]


def solution(mesh):
    in_specs = (
        P("row", "col", None, None),
        P("row", "col", None),
        P("row", "col", None, None),
        P("col", "row", None),
        P(),
        P(),
        P(),
    )
    out_specs = (P("row", "col", None, None), P("col", "row", None))
    body = functools.partial(shards, mesh.shape["row"], mesh.shape["col"])
    return jax.shard_map(body, mesh=mesh, in_specs=in_specs, out_specs=out_specs, check_vma=False)
```

```python
import functools
import math

import jax
import jax.numpy as jnp
from jax import lax
from jax.experimental import pallas as pl
from jax.experimental.pallas import tpu as pltpu
from jax.sharding import PartitionSpec as P

OFFSETS = (0, 0, 1, -1, 2, -2, 3, -3)
ROOT_HALF = 0.7071067811865476
PARTS = 2
PIECES = 4
ORDER = (0, 3, 2, 1)
MESH = pl.DeviceIdType.MESH
F32 = jnp.float32
BF16 = jnp.bfloat16


def silu(v):
    half = 0.5 * v
    return half + half * jnp.tanh(half)


def mm(a, b):
    return jnp.dot(a, b, preferred_element_type=F32)


def kernel(
    rows_n,
    cols_n,
    msg_hbm,
    tgt_hbm,
    rev_hbm,
    node_hbm,
    w_in_hbm,
    w_res_hbm,
    w_node_hbm,
    edge_out,
    node_out,
    w_in,
    w_res,
    w_node,
    tgt,
    rev,
    msg,
    cur,
    hot_part,
    acc,
    onehot,
    onehot_sent,
    perm,
    m_sent,
    base,
    pre,
    h_own,
    h_all,
    part_out,
    part_in,
    u_out,
    u_in,
    w_sem,
    rs_send,
    rs_recv,
    ag_send,
    ag_recv,
    col_send,
    col_recv,
    in_sem,
    out_sem,
):
    r, c = lax.axis_index("row"), lax.axis_index("col")
    edges, feat = msg_hbm.shape
    share = node_hbm.shape[0]
    points = share * rows_n
    blocks = len(OFFSETS)
    block = edges // blocks
    pair = 2 * block
    pairs = edges // pair
    group = points // PARTS
    piece = share // PARTS
    agg_scale = 1.0 / math.sqrt(edges // share)
    layers = w_in_hbm.shape[0]
    along_x = rows_n // 2
    r_y, r_x = r // along_x, lax.rem(r, along_x)
    steps = [(dx, dy) for dy in (1, 0) for dx in (2, 1, 3, 0)]
    others = rows_n - 1

    def row_peer(j, sign=1):
        dx, dy = steps[j]
        x = lax.rem(r_x + along_x + sign * dx, along_x)
        return lax.rem(r_y + dy, 2) * along_x + x

    def col_peer(offset):
        return lax.rem(c + offset + cols_n, cols_n)

    def rows_of(device, part):
        return pl.ds(pl.multiple_of(device * share + part * piece, piece), piece)

    barrier = pltpu.get_barrier_semaphore()
    for j in range(others):
        pl.semaphore_signal(barrier, inc=1, device_id=(row_peer(j), c), device_id_type=MESH)
    for off in OFFSETS[2:]:
        pl.semaphore_signal(barrier, inc=1, device_id=(r, col_peer(off)), device_id_type=MESH)

    firsts = []
    for i, (src, dst) in enumerate(
        ((tgt_hbm, tgt), (msg_hbm, msg), (rev_hbm, rev), (node_hbm, h_own))
    ):
        firsts.append(pltpu.make_async_copy(src, dst, in_sem.at[i]))
        firsts[-1].start()
    def rs_copy(t, part, j):
        return pltpu.make_async_remote_copy(
            src_ref=part_out.at[t, part, j],
            dst_ref=part_in.at[t, part, j],
            send_sem=rs_send.at[t, part],
            recv_sem=rs_recv.at[t, part],
            device_id=(row_peer(j), c),
            device_id_type=MESH,
        )

    def ag_copy(t, part, j):
        target = h_all.at[t, rows_of(r, part)]
        return pltpu.make_async_remote_copy(
            src_ref=target,
            dst_ref=target,
            send_sem=ag_send.at[t, part],
            recv_sem=ag_recv.at[t, part],
            device_id=(row_peer(j), c),
            device_id_type=MESH,
        )

    def rs_all(t, part):
        return pltpu.make_async_remote_copy(
            src_ref=part_out.at[t, part],
            dst_ref=part_in.at[t, part],
            send_sem=rs_send.at[t, part],
            recv_sem=rs_recv.at[t, part],
            device_id=(row_peer(0), c),
            device_id_type=MESH,
        )

    def ag_all(t, part):
        rows = h_all.at[t, pl.ds(0, others * piece)]
        return pltpu.make_async_remote_copy(
            src_ref=rows,
            dst_ref=rows,
            send_sem=ag_send.at[t, part],
            recv_sem=ag_recv.at[t, part],
            device_id=(row_peer(0), c),
            device_id_type=MESH,
        )

    def blocks_of(q):
        return (2 * q, 2 * q + 1) if q else ()

    def col_copy(t, b):
        return pltpu.make_async_remote_copy(
            src_ref=u_out.at[t, b],
            dst_ref=u_in.at[t, (b ^ 1) - 2],
            send_sem=col_send.at[t, b // 2],
            recv_sem=col_recv.at[t, b // 2],
            device_id=(r, col_peer(OFFSETS[b])),
            device_id_type=MESH,
        )

    def col_both(t, q):
        return pltpu.make_async_remote_copy(
            src_ref=u_out.at[t, pl.ds(2 * q, 2)],
            dst_ref=u_in.at[t, pl.ds(2 * q - 2, 2)],
            send_sem=col_send.at[t, q],
            recv_sem=col_recv.at[t, q],
            device_id=(r, col_peer(OFFSETS[2 * q])),
            device_id_type=MESH,
        )

    def send_sums(t, part, sums):
        for j in range(others):
            part_out[t, part, j] = sums[j * piece : (j + 1) * piece].astype(BF16)
            if t == 0 and part == 0 and j == 0:
                pl.semaphore_wait(barrier, others + blocks - 2)
            rs_copy(t, part, j).start()
        acc[part * group + others * piece : (part + 1) * group] = sums[others * piece :]

    firsts[0].wait()
    for part in range(PARTS):
        for j in range(rows_n):
            ids = lax.broadcasted_iota(jnp.int32, (piece, edges), 0) + (
                row_peer(j) * share + part * piece
            )
            first = part * group + j * piece
            hot_part[first : first + piece] = jnp.where(tgt[...] == ids, 1.0, 0.0).astype(BF16)
        if part == 0:
            firsts[1].wait()
        send_sums(0, part, mm(hot_part[part * group : (part + 1) * group], msg[...]))

    loads = []
    for t in range(layers):
        for i, (src, dst) in enumerate(
            ((w_in_hbm, w_in), (w_node_hbm, w_node), (w_res_hbm, w_res))
        ):
            loads.append(pltpu.make_async_copy(src.at[t], dst.at[t], w_sem.at[t, i]))
            loads[-1].start()

    firsts[2].wait()
    lane = lax.broadcasted_iota(jnp.int32, (block, block), 1)
    sublane = lax.broadcasted_iota(jnp.int32, (block, block), 0)
    for k in range(blocks):
        rows = pl.ds(k * block, block)
        ids = jnp.broadcast_to(tgt[0:1, k * block : (k + 1) * block], (block, block)).T
        for i in range(points // block):
            onehot[rows, i * block : (i + 1) * block] = jnp.where(
                ids == lane + i * block, 1.0, 0.0
            ).astype(BF16)
        ids = jnp.broadcast_to(rev[k : k + 1, :], (block, block))
        perm[k] = jnp.where(ids == sublane, 1.0, 0.0).astype(BF16)
        onehot_sent[rows] = mm(perm[k], onehot[rows]).astype(BF16)

    firsts[3].wait()
    edge_copies = []
    for t in range(layers):
        last = t == layers - 1
        held = msg if t == 0 else cur
        loads[3 * t].wait()
        for k in range(blocks):
            rows = pl.ds(k * block, block)
            m_sent[rows] = mm(perm[k], held[rows]).astype(BF16)
        for q in range(pairs):
            rows = pl.ds(q * pair, pair)
            base[rows] = mm(m_sent[rows], w_in[t, :feat])

        loads[3 * t + 1].wait()
        for part in range(PARTS):
            total = acc[part * group + others * piece : (part + 1) * group]
            rs_all(t, part).wait_recv()
            for j in range(others):
                total = total + part_in[t, part, j].astype(F32)
            scaled = (total * agg_scale).astype(BF16)
            mine = slice(part * piece, (part + 1) * piece)
            h_new = (h_own[mine].astype(F32) + silu(mm(scaled, w_node[t]))).astype(BF16)
            h_own[mine] = h_new
            h_all[t, rows_of(r, part)] = h_new
            for j in range(others):
                ag_copy(t, part, j).start()
        if last:
            node_copy = pltpu.make_async_copy(h_own, node_out, out_sem.at[pairs])
            node_copy.start()
        for part in range(PARTS):
            ag_all(t, part).wait_recv()

        for q in (3, 2, 1, 0):
            rows = pl.ds(q * pair, pair)
            picked = mm(onehot_sent[rows], h_all[t]).astype(BF16)
            u = (base[rows] + mm(picked, w_in[t, feat : 2 * feat])).astype(BF16)
            for i in range(2):
                u_out[t, 2 * q + i] = u[i * block : (i + 1) * block]
            for b in blocks_of(q):
                col_copy(t, b).start()
        for q in ORDER:
            rows = pl.ds(q * pair, pair)
            picked = mm(onehot[rows], h_all[t]).astype(BF16)
            pre[rows] = mm(picked, w_in[t, 2 * feat :])

        loads[3 * t + 2].wait()
        def edge_layer(x1, m):
            hidden = silu(x1).astype(BF16)
            inner = silu(mm(hidden, w_res[t, 0, 0])).astype(BF16)
            hidden = (
                (hidden.astype(F32) + silu(mm(inner, w_res[t, 0, 1]))) * ROOT_HALF
            ).astype(BF16)
            inner = silu(mm(hidden, w_res[t, 1, 0])).astype(BF16)
            summed = (hidden.astype(F32) + silu(mm(inner, w_res[t, 1, 1]))) * ROOT_HALF
            return ((m.astype(F32) + summed) * ROOT_HALF).astype(BF16)

        for part in range(PARTS):
            rs_all(t, part).wait_send()
            ag_all(t, part).wait_send()
        if t:
            col_both(t - 1, ORDER[-1]).wait_send()
        for n, q in enumerate(ORDER):
            if n > 1:
                col_both(t, ORDER[n - 1]).wait_send()
            rows = pl.ds(q * pair, pair)
            arrived = []
            if q:
                col_both(t, q).wait_recv()
            for k in (2 * q, 2 * q + 1):
                arrived.append(u_in[t, k - 2] if q else u_out[t, k ^ 1])
            sums = pre[rows] + jnp.concatenate(arrived, axis=0).astype(F32)
            cur[rows] = edge_layer(sums, held[rows])
            if last:
                edge_copies.append(
                    pltpu.make_async_copy(cur.at[rows], edge_out.at[rows], out_sem.at[q])
                )
                edge_copies[-1].start()
            if last:
                continue
            columns = slice(q * pair, (q + 1) * pair)
            for part in range(PARTS):
                points_of = pl.ds(part * group, group)
                sums = mm(hot_part[points_of, columns], cur[rows])
                if q != ORDER[0]:
                    sums = acc[points_of] + sums
                if q == ORDER[-1]:
                    send_sums(t + 1, part, sums)
                else:
                    acc[points_of] = sums

    col_both(layers - 1, ORDER[-1]).wait_send()
    for copy in edge_copies:
        copy.wait()
    node_copy.wait()


def hand_over(edge_in, node_in, edge_out, node_out, edge_held, node_held, sems):
    piece = edge_in.shape[0] // PIECES
    moves = [(node_in, node_held, node_out)]
    for i in range(PIECES):
        rows = pl.ds(i * piece, piece)
        moves.append((edge_in.at[rows], edge_held.at[rows], edge_out.at[rows]))
    loads = [pltpu.make_async_copy(m[0], m[1], sems.at[0, i]) for i, m in enumerate(moves)]
    stores = [pltpu.make_async_copy(m[1], m[2], sems.at[1, i]) for i, m in enumerate(moves)]
    for copy in loads:
        copy.start()
    for load, store in zip(loads, stores):
        load.wait()
        store.start()
    for copy in stores:
        copy.wait()


def shards(rows_n, cols_n, messages, targets, reverse_rows, nodes, w_in, w_res, w_node):
    msg, tgt, rev, node = messages[0, 0], targets[0], reverse_rows[0, 0], nodes[0]
    edges, feat = msg.shape
    share = node.shape[0]
    points = share * rows_n
    layers = w_in.shape[0]
    blocks = len(OFFSETS)
    block = edges // blocks
    dma = pltpu.SemaphoreType.DMA
    hbm = pl.BlockSpec(memory_space=pltpu.HBM)
    shapes = (
        jax.ShapeDtypeStruct((edges, feat), BF16),
        jax.ShapeDtypeStruct((share, feat), BF16),
    )
    held = pl.pallas_call(
        functools.partial(kernel, rows_n, cols_n),
        out_shape=shapes,
        in_specs=[hbm] * 7,
        out_specs=(hbm, hbm),
        scratch_shapes=[
            pltpu.VMEM(w_in.shape, BF16),
            pltpu.VMEM(w_res.shape, BF16),
            pltpu.VMEM(w_node.shape, BF16),
            pltpu.VMEM(tgt.shape, tgt.dtype),
            pltpu.VMEM(rev.shape, rev.dtype),
            pltpu.VMEM((edges, feat), BF16),
            pltpu.VMEM((edges, feat), BF16),
            pltpu.VMEM((points, edges), BF16),
            pltpu.VMEM((points, feat), F32),
            pltpu.VMEM((edges, points), BF16),
            pltpu.VMEM((edges, points), BF16),
            pltpu.VMEM((blocks, block, block), BF16),
            pltpu.VMEM((edges, feat), BF16),
            pltpu.VMEM((edges, feat), F32),
            pltpu.VMEM((edges, feat), F32),
            pltpu.VMEM((share, feat), BF16),
            pltpu.VMEM((layers, points, feat), BF16),
            pltpu.VMEM((layers, PARTS, rows_n - 1, share // PARTS, feat), BF16),
            pltpu.VMEM((layers, PARTS, rows_n - 1, share // PARTS, feat), BF16),
            pltpu.VMEM((layers, blocks, block, feat), BF16),
            pltpu.VMEM((layers, blocks - 2, block, feat), BF16),
            dma((layers, 3)),
            dma((layers, PARTS)),
            dma((layers, PARTS)),
            dma((layers, PARTS)),
            dma((layers, PARTS)),
            dma((layers, blocks // 2)),
            dma((layers, blocks // 2)),
            dma((4,)),
            dma((blocks // 2 + 1,)),
        ],
        compiler_params=pltpu.CompilerParams(
            collective_id=0, has_side_effects=True, vmem_limit_bytes=56 * 2**20
        ),
        cost_estimate=pl.CostEstimate(
            flops=11 * 10**9, bytes_accessed=12 * 10**6, transcendentals=5 * 10**6
        ),
    )(msg, tgt, rev, node, w_in, w_res, w_node)
    edge_out, node_out = pl.pallas_call(
        hand_over,
        out_shape=shapes,
        in_specs=[hbm] * 2,
        out_specs=(hbm, hbm),
        scratch_shapes=[pltpu.VMEM((edges, feat), BF16), pltpu.VMEM((share, feat), BF16), dma((2, PIECES + 1))],
    )(*held)
    return edge_out[None, None], node_out[None]


def solution(mesh):
    in_specs = (
        P("row", "col", None, None),
        P("row", "col", None),
        P("row", "col", None, None),
        P("col", "row", None),
        P(),
        P(),
        P(),
    )
    out_specs = (P("row", "col", None, None), P("col", "row", None))
    body = functools.partial(shards, mesh.shape["row"], mesh.shape["col"])
    return jax.shard_map(body, mesh=mesh, in_specs=in_specs, out_specs=out_specs, check_vma=False)
```

```python
import functools
import math

import jax
import jax.numpy as jnp
from jax import lax
from jax.experimental import pallas as pl
from jax.experimental.pallas import tpu as pltpu
from jax.sharding import PartitionSpec as P

OFFSETS = (0, 0, 1, -1, 2, -2, 3, -3)
ROOT_HALF = 0.7071067811865476
PARTS = 2
PIECES = 4
ORDER = (0, 3, 2, 1)
MESH = pl.DeviceIdType.MESH
F32 = jnp.float32
BF16 = jnp.bfloat16


def silu(v):
    half = 0.5 * v
    return half + half * jnp.tanh(half)


def mm(a, b):
    return jnp.dot(a, b, preferred_element_type=F32)


def kernel(
    rows_n,
    cols_n,
    msg_hbm,
    tgt_hbm,
    rev_hbm,
    node_hbm,
    w_in_hbm,
    w_res_hbm,
    w_node_hbm,
    edge_out,
    node_out,
    w_in,
    w_res,
    w_node,
    tgt,
    rev,
    msg,
    cur,
    hot_part,
    acc,
    onehot,
    onehot_sent,
    perm,
    m_sent,
    base,
    pre,
    h_own,
    h_all,
    part_out,
    part_in,
    u_out,
    u_in,
    w_sem,
    rs_send,
    rs_recv,
    ag_send,
    ag_recv,
    col_send,
    col_recv,
    in_sem,
    out_sem,
):
    r, c = lax.axis_index("row"), lax.axis_index("col")
    edges, feat = msg_hbm.shape
    share = node_hbm.shape[0]
    points = share * rows_n
    blocks = len(OFFSETS)
    block = edges // blocks
    pair = 2 * block
    pairs = edges // pair
    group = points // PARTS
    piece = share // PARTS
    agg_scale = 1.0 / math.sqrt(edges // share)
    layers = w_in_hbm.shape[0]
    along_x = rows_n // 2
    r_y, r_x = r // along_x, lax.rem(r, along_x)
    steps = [(dx, dy) for dy in (1, 0) for dx in (2, 1, 3, 0)]
    others = rows_n - 1

    def row_peer(j, sign=1):
        dx, dy = steps[j]
        x = lax.rem(r_x + along_x + sign * dx, along_x)
        return lax.rem(r_y + dy, 2) * along_x + x

    def col_peer(offset):
        return lax.rem(c + offset + cols_n, cols_n)

    def rows_of(device, part):
        return pl.ds(pl.multiple_of(device * share + part * piece, piece), piece)

    firsts = []
    for i, (src, dst) in enumerate(
        ((tgt_hbm, tgt), (msg_hbm, msg), (rev_hbm, rev), (node_hbm, h_own))
    ):
        firsts.append(pltpu.make_async_copy(src, dst, in_sem.at[i]))
        firsts[-1].start()
    barrier = pltpu.get_barrier_semaphore()
    for j in range(others):
        pl.semaphore_signal(barrier, inc=1, device_id=(row_peer(j), c), device_id_type=MESH)
    for off in OFFSETS[2:]:
        pl.semaphore_signal(barrier, inc=1, device_id=(r, col_peer(off)), device_id_type=MESH)

    def rs_copy(t, part, j):
        return pltpu.make_async_remote_copy(
            src_ref=part_out.at[t, part, j],
            dst_ref=part_in.at[t, part, j],
            send_sem=rs_send.at[t, part],
            recv_sem=rs_recv.at[t, part],
            device_id=(row_peer(j), c),
            device_id_type=MESH,
        )

    def ag_copy(t, part, j):
        target = h_all.at[t, rows_of(r, part)]
        return pltpu.make_async_remote_copy(
            src_ref=target,
            dst_ref=target,
            send_sem=ag_send.at[t, part],
            recv_sem=ag_recv.at[t, part],
            device_id=(row_peer(j), c),
            device_id_type=MESH,
        )

    def rs_all(t, part):
        return pltpu.make_async_remote_copy(
            src_ref=part_out.at[t, part],
            dst_ref=part_in.at[t, part],
            send_sem=rs_send.at[t, part],
            recv_sem=rs_recv.at[t, part],
            device_id=(row_peer(0), c),
            device_id_type=MESH,
        )

    def ag_all(t, part):
        rows = h_all.at[t, pl.ds(0, others * piece)]
        return pltpu.make_async_remote_copy(
            src_ref=rows,
            dst_ref=rows,
            send_sem=ag_send.at[t, part],
            recv_sem=ag_recv.at[t, part],
            device_id=(row_peer(0), c),
            device_id_type=MESH,
        )

    def blocks_of(q):
        return (2 * q, 2 * q + 1) if q else ()

    def col_copy(t, b):
        return pltpu.make_async_remote_copy(
            src_ref=u_out.at[t, b],
            dst_ref=u_in.at[t, (b ^ 1) - 2],
            send_sem=col_send.at[t, b // 2],
            recv_sem=col_recv.at[t, b // 2],
            device_id=(r, col_peer(OFFSETS[b])),
            device_id_type=MESH,
        )

    def col_both(t, q):
        return pltpu.make_async_remote_copy(
            src_ref=u_out.at[t, pl.ds(2 * q, 2)],
            dst_ref=u_in.at[t, pl.ds(2 * q - 2, 2)],
            send_sem=col_send.at[t, q],
            recv_sem=col_recv.at[t, q],
            device_id=(r, col_peer(OFFSETS[2 * q])),
            device_id_type=MESH,
        )

    def send_sums(t, part, sums):
        for j in range(others):
            part_out[t, part, j] = sums[j * piece : (j + 1) * piece].astype(BF16)
            if t == 0 and part == 0 and j == 0:
                pl.semaphore_wait(barrier, others + blocks - 2)
            rs_copy(t, part, j).start()
        acc[part * group + others * piece : (part + 1) * group] = sums[others * piece :]

    firsts[0].wait()
    for part in range(PARTS):
        for j in range(rows_n):
            ids = lax.broadcasted_iota(jnp.int32, (piece, edges), 0) + (
                row_peer(j) * share + part * piece
            )
            first = part * group + j * piece
            hot_part[first : first + piece] = jnp.where(tgt[...] == ids, 1.0, 0.0).astype(BF16)
        if part == 0:
            firsts[1].wait()
        send_sums(0, part, mm(hot_part[part * group : (part + 1) * group], msg[...]))

    loads = []
    for t in range(layers):
        for i, (src, dst) in enumerate(
            ((w_in_hbm, w_in), (w_node_hbm, w_node), (w_res_hbm, w_res))
        ):
            loads.append(pltpu.make_async_copy(src.at[t], dst.at[t], w_sem.at[t, i]))
            loads[-1].start()

    firsts[2].wait()
    lane = lax.broadcasted_iota(jnp.int32, (block, block), 1)
    sublane = lax.broadcasted_iota(jnp.int32, (block, block), 0)
    for k in range(blocks):
        rows = pl.ds(k * block, block)
        ids = jnp.broadcast_to(tgt[0:1, k * block : (k + 1) * block], (block, block)).T
        for i in range(points // block):
            onehot[rows, i * block : (i + 1) * block] = jnp.where(
                ids == lane + i * block, 1.0, 0.0
            ).astype(BF16)
        ids = jnp.broadcast_to(rev[k : k + 1, :], (block, block))
        perm[k] = jnp.where(ids == sublane, 1.0, 0.0).astype(BF16)
        onehot_sent[rows] = mm(perm[k], onehot[rows]).astype(BF16)

    firsts[3].wait()
    edge_copies = []
    for t in range(layers):
        last = t == layers - 1
        held = msg if t == 0 else cur
        loads[3 * t].wait()
        for k in range(blocks):
            rows = pl.ds(k * block, block)
            m_sent[rows] = mm(perm[k], held[rows]).astype(BF16)
        for q in range(pairs):
            rows = pl.ds(q * pair, pair)
            base[rows] = mm(m_sent[rows], w_in[t, :feat])

        loads[3 * t + 1].wait()
        for part in range(PARTS):
            total = acc[part * group + others * piece : (part + 1) * group]
            rs_all(t, part).wait_recv()
            for j in range(others):
                total = total + part_in[t, part, j].astype(F32)
            scaled = (total * agg_scale).astype(BF16)
            mine = slice(part * piece, (part + 1) * piece)
            h_new = (h_own[mine].astype(F32) + silu(mm(scaled, w_node[t]))).astype(BF16)
            h_own[mine] = h_new
            h_all[t, rows_of(r, part)] = h_new
            for j in range(others):
                ag_copy(t, part, j).start()
        if last:
            node_copy = pltpu.make_async_copy(h_own, node_out, out_sem.at[pairs])
            node_copy.start()
        for part in range(PARTS):
            ag_all(t, part).wait_recv()

        for q in (3, 2, 1, 0):
            rows = pl.ds(q * pair, pair)
            picked = mm(onehot_sent[rows], h_all[t]).astype(BF16)
            u = (base[rows] + mm(picked, w_in[t, feat : 2 * feat])).astype(BF16)
            for i in range(2):
                u_out[t, 2 * q + i] = u[i * block : (i + 1) * block]
            for b in blocks_of(q):
                col_copy(t, b).start()
        for q in ORDER:
            rows = pl.ds(q * pair, pair)
            picked = mm(onehot[rows], h_all[t]).astype(BF16)
            pre[rows] = mm(picked, w_in[t, 2 * feat :])

        loads[3 * t + 2].wait()
        def edge_layer(x1, m):
            hidden = silu(x1).astype(BF16)
            inner = silu(mm(hidden, w_res[t, 0, 0])).astype(BF16)
            hidden = (
                (hidden.astype(F32) + silu(mm(inner, w_res[t, 0, 1]))) * ROOT_HALF
            ).astype(BF16)
            inner = silu(mm(hidden, w_res[t, 1, 0])).astype(BF16)
            summed = (hidden.astype(F32) + silu(mm(inner, w_res[t, 1, 1]))) * ROOT_HALF
            return ((m.astype(F32) + summed) * ROOT_HALF).astype(BF16)

        for part in range(PARTS):
            rs_all(t, part).wait_send()
            ag_all(t, part).wait_send()
        if t:
            col_both(t - 1, ORDER[-1]).wait_send()
        for n, q in enumerate(ORDER):
            if n > 1:
                col_both(t, ORDER[n - 1]).wait_send()
            rows = pl.ds(q * pair, pair)
            arrived = []
            if q:
                col_both(t, q).wait_recv()
            for k in (2 * q, 2 * q + 1):
                arrived.append(u_in[t, k - 2] if q else u_out[t, k ^ 1])
            sums = pre[rows] + jnp.concatenate(arrived, axis=0).astype(F32)
            cur[rows] = edge_layer(sums, held[rows])
            if last:
                edge_copies.append(
                    pltpu.make_async_copy(cur.at[rows], edge_out.at[rows], out_sem.at[q])
                )
                edge_copies[-1].start()
            if last:
                continue
            columns = slice(q * pair, (q + 1) * pair)
            for part in range(PARTS):
                points_of = pl.ds(part * group, group)
                sums = mm(hot_part[points_of, columns], cur[rows])
                if q != ORDER[0]:
                    sums = acc[points_of] + sums
                if q == ORDER[-1]:
                    send_sums(t + 1, part, sums)
                else:
                    acc[points_of] = sums

    col_both(layers - 1, ORDER[-1]).wait_send()
    for copy in edge_copies:
        copy.wait()
    node_copy.wait()


def hand_over(edge_in, node_in, edge_out, node_out, edge_held, node_held, sems):
    piece = edge_in.shape[0] // PIECES
    moves = [(node_in, node_held, node_out)]
    for i in range(PIECES):
        rows = pl.ds(i * piece, piece)
        moves.append((edge_in.at[rows], edge_held.at[rows], edge_out.at[rows]))
    loads = [pltpu.make_async_copy(m[0], m[1], sems.at[0, i]) for i, m in enumerate(moves)]
    stores = [pltpu.make_async_copy(m[1], m[2], sems.at[1, i]) for i, m in enumerate(moves)]
    for copy in loads:
        copy.start()
    for load, store in zip(loads, stores):
        load.wait()
        store.start()
    for copy in stores:
        copy.wait()


def shards(rows_n, cols_n, messages, targets, reverse_rows, nodes, w_in, w_res, w_node):
    msg, tgt, rev, node = messages[0, 0], targets[0], reverse_rows[0, 0], nodes[0]
    edges, feat = msg.shape
    share = node.shape[0]
    points = share * rows_n
    layers = w_in.shape[0]
    blocks = len(OFFSETS)
    block = edges // blocks
    dma = pltpu.SemaphoreType.DMA
    hbm = pl.BlockSpec(memory_space=pltpu.HBM)
    shapes = (
        jax.ShapeDtypeStruct((edges, feat), BF16),
        jax.ShapeDtypeStruct((share, feat), BF16),
    )
    held = pl.pallas_call(
        functools.partial(kernel, rows_n, cols_n),
        out_shape=shapes,
        in_specs=[hbm] * 7,
        out_specs=(hbm, hbm),
        scratch_shapes=[
            pltpu.VMEM(w_in.shape, BF16),
            pltpu.VMEM(w_res.shape, BF16),
            pltpu.VMEM(w_node.shape, BF16),
            pltpu.VMEM(tgt.shape, tgt.dtype),
            pltpu.VMEM(rev.shape, rev.dtype),
            pltpu.VMEM((edges, feat), BF16),
            pltpu.VMEM((edges, feat), BF16),
            pltpu.VMEM((points, edges), BF16),
            pltpu.VMEM((points, feat), F32),
            pltpu.VMEM((edges, points), BF16),
            pltpu.VMEM((edges, points), BF16),
            pltpu.VMEM((blocks, block, block), BF16),
            pltpu.VMEM((edges, feat), BF16),
            pltpu.VMEM((edges, feat), F32),
            pltpu.VMEM((edges, feat), F32),
            pltpu.VMEM((share, feat), BF16),
            pltpu.VMEM((layers, points, feat), BF16),
            pltpu.VMEM((layers, PARTS, rows_n - 1, share // PARTS, feat), BF16),
            pltpu.VMEM((layers, PARTS, rows_n - 1, share // PARTS, feat), BF16),
            pltpu.VMEM((layers, blocks, block, feat), BF16),
            pltpu.VMEM((layers, blocks - 2, block, feat), BF16),
            dma((layers, 3)),
            dma((layers, PARTS)),
            dma((layers, PARTS)),
            dma((layers, PARTS)),
            dma((layers, PARTS)),
            dma((layers, blocks // 2)),
            dma((layers, blocks // 2)),
            dma((4,)),
            dma((blocks // 2 + 1,)),
        ],
        compiler_params=pltpu.CompilerParams(
            collective_id=0, has_side_effects=True, vmem_limit_bytes=56 * 2**20
        ),
        cost_estimate=pl.CostEstimate(
            flops=11 * 10**9, bytes_accessed=12 * 10**6, transcendentals=5 * 10**6
        ),
    )(msg, tgt, rev, node, w_in, w_res, w_node)
    edge_out, node_out = pl.pallas_call(
        hand_over,
        out_shape=shapes,
        in_specs=[hbm] * 2,
        out_specs=(hbm, hbm),
        scratch_shapes=[pltpu.VMEM((edges, feat), BF16), pltpu.VMEM((share, feat), BF16), dma((2, PIECES + 1))],
    )(*held)
    return edge_out[None, None], node_out[None]


def solution(mesh):
    in_specs = (
        P("row", "col", None, None),
        P("row", "col", None),
        P("row", "col", None, None),
        P("col", "row", None),
        P(),
        P(),
        P(),
    )
    out_specs = (P("row", "col", None, None), P("col", "row", None))
    body = functools.partial(shards, mesh.shape["row"], mesh.shape["col"])
    return jax.shard_map(body, mesh=mesh, in_specs=in_specs, out_specs=out_specs, check_vma=False)
```
